128 devices in a mesh: owner: 16 (over y, z), suf: 8 (over x, core).
Axes of the slice: x: 4, y: 4, z: 4, core: 2. Of those that a mesh axis runs over, the one named last changes fastest.
Arguments:
- queries: bfloat16 [512, 2, 8192], P('owner', None, 'suf'), may hold values from -40 to 40
- new_keys: bfloat16 [512, 2, 1024], P('owner', None, 'suf'), may hold values from -40 to 40
- new_values: bfloat16 [512, 2, 1024], P('owner', None, 'suf'), may hold values from -6 to 6
- prompt_keys: bfloat16 [16, 8, 8192, 128], P('owner', 'suf'), may hold values from -6 to 6
- prompt_values: bfloat16 [16, 8, 8192, 128], P('owner', 'suf'), may hold values from -6 to 6
- suffix_keys: bfloat16 [512, 256, 1024], P('owner', None, 'suf'), may hold values from -9.5625 to 9.5625
- suffix_values: bfloat16 [512, 256, 1024], P('owner', None, 'suf'), may hold values from -6 to 6
- suffix_len: int32 [512], P('owner'), may hold values from 1 to 256, 65536 in all
- prompt_of_row: int32 [512], P('owner'), may hold values from 0 to 15, as said below
- partner: int32 [512], P('owner'), may hold values from 0 to 511, as said below
- out_weight: bfloat16 [8192, 8192], P(None, 'suf'), may hold values from -0.0625 to 0.0625
Outputs:
- layer_out: bfloat16 [512, 2, 8192], P('owner', None, 'suf')
The draws below stay inside these ranges and needn't reach their ends.
Inputs may be any that keep to these rules, and one draw needn't show every extreme that they name: `prompt_of_row`: among the 32 rows of one index of owner, no prompt is named by more than 8 rows, and on every index some prompt is named by exactly 8 rows. partner[r] lies among the 32 rows of the same index of owner as r and has the same prompt as r; it may be r itself.
All inputs are finite; a program needn't handle non-finite values. No bound on the sum of `suffix_len` on one device may be relied on, other than what follows from the above.
Results may differ from the reference program's by a relative error of at most 0.005.
Values may be sent and summed in bfloat16 or wider, within the bound.
A program may use at most 128 MiB of HBM per device.

```python
import math
import jax
import jax.numpy as jnp
import numpy as np
from jax import lax

D = 8192
H = 64
KVH = 8
HD = 128
STEPS = 2
ROW_DEV = 32
PROMPT_LEN = 8192
SUF_LEN = 256
GROUP = 8
CAP = 8
PROMPTS = 16
ROWS = 512


def prompt_table(key):
    base_key = jax.random.fold_in(key, 11)
    key_hot, key_second, key_offset, key_order = jax.random.split(base_key, 4)
    hot_prompt = jax.random.randint(key_hot, (), 0, PROMPTS)
    second_prompt = (hot_prompt + 1 + jax.random.randint(key_second, (PROMPTS, 1), 0, PROMPTS - 1)) % PROMPTS
    offsets = jax.random.randint(key_offset, (PROMPTS, 1), 0, PROMPTS - 1)
    position = jnp.arange(ROW_DEV, dtype=jnp.int32)[None, :]
    spread = (hot_prompt + 1 + (offsets + position) % (PROMPTS - 1)) % PROMPTS
    drawn = jnp.where(position < CAP, hot_prompt, jnp.where(position < CAP + CAP // 2, second_prompt, spread))
    order_scores = jax.random.randint(key_order, (PROMPTS, ROW_DEV), 0, 1 << 20) * ROW_DEV + position
    order = jnp.argsort(order_scores, axis=1, stable=True)
    return jnp.take_along_axis(drawn, order, axis=1).astype(jnp.int32)


def draw_prompt_of_row(key, part):
    return prompt_table(key).reshape(ROWS).astype(jnp.int32)


def draw_partner(key, part):
    table = prompt_table(key)
    key_pick = jax.random.fold_in(key, 23)
    position = jnp.arange(ROW_DEV, dtype=jnp.int32)
    same_prompt = table[:, :, None] == table[:, None, :]
    pick_scores = jax.random.randint(key_pick, (PROMPTS, ROW_DEV, ROW_DEV), 0, 1 << 16) * ROW_DEV + position[None, None, :]
    masked = jnp.where(same_prompt, pick_scores, -1)
    chosen = jnp.argmax(masked, axis=2).astype(jnp.int32)
    return (jnp.arange(PROMPTS, dtype=jnp.int32)[:, None] * ROW_DEV + chosen).reshape(ROWS).astype(jnp.int32)


def drawn_pair(key):
    base_key = jax.random.fold_in(key, 5)
    key_shared, key_query, key_noise = jax.random.split(base_key, 3)
    shared = jax.random.normal(key_shared, (ROWS, 1, KVH, 1, HD), jnp.float32)
    query_part = shared + jax.random.normal(key_query, (ROWS, STEPS, KVH, GROUP, HD), jnp.float32)
    strength = (0.75 + 0.05 * jnp.arange(STEPS, dtype=jnp.float32)).reshape(1, STEPS, 1, 1, 1)
    key_part = strength * shared + 0.5 * jax.random.normal(key_noise, (ROWS, STEPS, KVH, 1, HD), jnp.float32)
    query_part = jnp.clip(query_part, -40.0, 40.0).reshape(ROWS, STEPS, H * HD)
    key_part = jnp.clip(key_part, -40.0, 40.0).reshape(ROWS, STEPS, KVH * HD)
    return (query_part, key_part)


def draw_queries(key, part):
    return drawn_pair(key)[0].astype(jnp.bfloat16)


def draw_new_keys(key, part):
    return drawn_pair(key)[1].astype(jnp.bfloat16)


def shard_levels(own_key, extent, cuts, smallest, top_value):
    def one(dim, parts):
        draws = jax.random.uniform(jax.random.fold_in(jax.random.fold_in(own_key, 6), dim), (parts,), jnp.float32, smallest / len(cuts), top_value / len(cuts))
        return jnp.repeat(jnp.exp(draws), extent[dim] // parts).reshape((-1,) + (1,) * (len(extent) - dim - 1))

    loudness = one(*cuts[0])
    for cut in cuts[1:]:
        loudness = loudness * one(*cut)
    return loudness


def length_profile(amount, total, limit, skew):
    weights = [(1 << 20) // math.isqrt(rank ** skew) + 1 for rank in range(2, amount + 1)]
    surplus, counts = total - limit - (amount - 1), [1] * (amount - 1)
    while surplus > 0:
        candidates = [i for i in range(amount - 1) if counts[i] < limit]
        whole, budget = sum([weights[i] for i in candidates]), surplus
        for i in candidates:
            extra = min(limit - counts[i], max(1, budget * weights[i] // whole), surplus)
            counts[i] = counts[i] + extra
            surplus = surplus - extra
    return np.array([limit] + counts)


def uneven_parts(stream_key, number_of, total, reach, skew):
    if number_of == 2:
        one = jax.random.randint(stream_key, (), max(1, total - reach), min(reach, total - 1) + 1)
        return jnp.stack([one, total - one])
    sizes = jnp.asarray(length_profile(number_of, total, reach, skew), jnp.int32)
    pairs = (number_of - 1) // 2
    giver, sink = sizes[1:1 + 2 * pairs:2], sizes[2:2 + 2 * pairs:2]
    slack = jnp.minimum(giver - 1, reach - sink)
    passed = jax.random.randint(jax.random.fold_in(stream_key, 1), (pairs,), 0, 1 << 20) % (slack + 1)
    sizes = sizes.at[1:1 + 2 * pairs:2].set(giver - passed).at[2:2 + 2 * pairs:2].set(sink + passed)
    return sizes[jax.random.permutation(jax.random.fold_in(stream_key, 2), number_of)]


def bell_draw(rng, extent, scale, bound, cuts=(), kind=jnp.bfloat16):
    factor_of = shard_levels(rng, extent, cuts, -0.22, 0.18) if cuts else 1.0
    array = jax.random.normal(rng, extent, jnp.float32) * scale * factor_of
    return jnp.minimum(jnp.maximum(array, -bound), bound).astype(kind)


def setup_inputs(seed: int = 0) -> dict:
    splits = jax.random.split(jax.random.key(seed), 12)
    queries = draw_queries(jax.random.fold_in(splits[11], 71), 0)
    new_keys = draw_new_keys(jax.random.fold_in(splits[11], 71), 0)
    new_values = bell_draw(splits[2], (ROWS, STEPS, KVH * HD), 1.0, 6.0, ((0, 16), (2, 8)))
    prompt_keys = bell_draw(splits[3], (PROMPTS, KVH, PROMPT_LEN, HD), 1.0, 6.0, ((0, 16), (1, 8)))
    prompt_values = bell_draw(splits[4], (PROMPTS, KVH, PROMPT_LEN, HD), 1.0, 6.0, ((0, 16), (1, 8)))
    suffix_keys = bell_draw(splits[5], (ROWS, SUF_LEN, KVH * HD), 1.6, 9.5625, ((0, 16), (2, 8)))
    suffix_values = bell_draw(splits[6], (ROWS, SUF_LEN, KVH * HD), 1.0, 6.0, ((0, 16), (2, 8)))
    suffix_len = uneven_parts(splits[7], ROWS, ROWS * SUF_LEN // 2, SUF_LEN, 2).astype(jnp.int32)
    prompt_of_row = draw_prompt_of_row(jax.random.fold_in(splits[11], 71), 0)
    partner = draw_partner(jax.random.fold_in(splits[11], 71), 0)
    out_weight = bell_draw(splits[10], (H * HD, D), (H * HD) ** -0.5, 0.0625, ((1, 8),))
    return {"queries": queries, "new_keys": new_keys, "new_values": new_values, "prompt_keys": prompt_keys, "prompt_values": prompt_values, "suffix_keys": suffix_keys, "suffix_values": suffix_values, "suffix_len": suffix_len, "prompt_of_row": prompt_of_row, "partner": partner, "out_weight": out_weight}


def rounded(weights):
    return lax.optimization_barrier(weights.astype(jnp.bfloat16)).astype(jnp.float32)


def attend(query_step, key_prompt, value_prompt, key_suffix, value_suffix, suffix_used, key_extra, value_extra):
    score_scale = HD ** -0.5
    prompt_scores = jnp.einsum("kgd,kld->kgl", query_step, key_prompt) * score_scale
    prompt_max = prompt_scores.max(-1)
    prompt_weights = jnp.exp(prompt_scores - prompt_max[..., None])
    prompt_sum = prompt_weights.sum(-1)
    prompt_weighted = jnp.einsum("kgl,kld->kgd", rounded(prompt_weights), value_prompt)
    prompt_part = rounded(prompt_weighted / prompt_sum[..., None])
    suffix_scores = jnp.einsum("kgd,skd->kgs", query_step, key_suffix) * score_scale
    extra_scores = jnp.einsum("kgd,ekd->kge", query_step, key_extra) * score_scale
    valid_mask = jnp.arange(SUF_LEN, dtype=jnp.int32) < suffix_used
    suffix_scores = jnp.where(valid_mask, suffix_scores, -1e30)
    local_max = jnp.maximum(suffix_scores.max(-1), extra_scores.max(-1))
    suffix_weights = jnp.where(valid_mask, jnp.exp(suffix_scores - local_max[..., None]), 0.0)
    extra_weights = jnp.exp(extra_scores - local_max[..., None])
    local_sum = suffix_weights.sum(-1) + extra_weights.sum(-1)
    local_part = jnp.einsum("kgs,skd->kgd", rounded(suffix_weights), value_suffix)
    local_part = local_part + jnp.einsum("kge,ekd->kgd", rounded(extra_weights), value_extra)
    top = jnp.maximum(prompt_max, local_max)
    prompt_scale = prompt_sum * jnp.exp(prompt_max - top)
    local_scale = jnp.exp(local_max - top)
    combined = prompt_part * prompt_scale[..., None] + local_part * local_scale[..., None]
    total = prompt_scale + local_sum * local_scale
    return (combined / total[..., None]).astype(jnp.bfloat16).reshape(-1)


def reference(queries, new_keys, new_values, prompt_keys, prompt_values, suffix_keys, suffix_values, suffix_len, prompt_of_row, partner, out_weight):
    def row_output(row_index):
        prompt_index = prompt_of_row[row_index]
        parent = partner[row_index]
        key_prompt = prompt_keys[prompt_index].astype(jnp.float32)
        value_prompt = prompt_values[prompt_index].astype(jnp.float32)
        query_row = queries[row_index].astype(jnp.float32).reshape(STEPS, KVH, GROUP, HD)
        own_keys = new_keys[row_index].astype(jnp.float32).reshape(STEPS, KVH, HD)
        own_values = new_values[row_index].astype(jnp.float32).reshape(STEPS, KVH, HD)
        parent_keys = new_keys[parent].astype(jnp.float32).reshape(STEPS, KVH, HD)
        parent_values = new_values[parent].astype(jnp.float32).reshape(STEPS, KVH, HD)
        own_suffix_keys = suffix_keys[row_index].astype(jnp.float32).reshape(SUF_LEN, KVH, HD)
        own_suffix_values = suffix_values[row_index].astype(jnp.float32).reshape(SUF_LEN, KVH, HD)
        parent_suffix_keys = suffix_keys[parent].astype(jnp.float32).reshape(SUF_LEN, KVH, HD)
        parent_suffix_values = suffix_values[parent].astype(jnp.float32).reshape(SUF_LEN, KVH, HD)
        first_step = attend(query_row[0], key_prompt, value_prompt, own_suffix_keys, own_suffix_values, suffix_len[row_index], own_keys[0:1], own_values[0:1])
        second_step = attend(query_row[1], key_prompt, value_prompt, parent_suffix_keys, parent_suffix_values, suffix_len[parent], jnp.stack([parent_keys[0], own_keys[1]]), jnp.stack([parent_values[0], own_values[1]]))
        return jnp.stack([first_step, second_step])

    attention = lax.map(row_output, jnp.arange(ROWS, dtype=jnp.int32))
    projected = jnp.dot(attention.reshape(ROWS * STEPS, H * HD), out_weight, preferred_element_type=jnp.float32)
    return projected.astype(jnp.bfloat16).reshape(ROWS, STEPS, D)
```

```python
import jax
import jax.numpy as jnp
from jax import lax
from jax.experimental import pallas as pl
from jax.experimental.pallas import tpu as pltpu
from jax.sharding import PartitionSpec as P

MESH = pl.DeviceIdType.MESH
HD = 128
GROUP = 8
CAP = 8
STEPS = 2
SIDE = 4
OWNERS = 16
SUFS = 8
ROWS = 32
SLOT = STEPS * GROUP
BLOCK = CAP * SLOT
LENGTH = 8192
SUFFIX = 256
WIDTH = GROUP * HD
SPAN = 1024
CHUNK = SIDE * BLOCK
SPANS = LENGTH // SPAN
RATE = HD ** (-0.5) * 1.4426950408889634
F32 = jnp.float32
BF16 = jnp.bfloat16


def dot_t(a, b):
    return lax.dot_general(a, b, (((1,), (1,)), ((), ())), preferred_element_type=F32)


def kernel(
    prompt_s, partner_s, length_s,
    q_hbm, nk_hbm, nv_hbm, ks_hbm, vs_hbm, k_hbm, v_hbm, w_hbm,
    out_ref,
    q_v, nk_v, nv_v, ks_v, vs_v, k_v, v_v, vt_v, w_v,
    table_v, table_s, pack_v, rq_v,
    s_v, m_v, l_v, acc_v,
    part_v, stat_v, back_v, bstat_v, bstat_t,
    e_v, pe_v, lo_v, lm_v, ls_v,
    att_v, ag_v, proj_v,
    load_sem, table_sem,
    qsend, qrecv, bsend, brecv, ssend, srecv, gsend, grecv,
):
    me = lax.axis_index("owner")
    lane_f = lax.axis_index("suf")
    y, z = me // SIDE, me % SIDE
    x, core = lane_f // 2, lane_f % 2

    barrier = pltpu.get_barrier_semaphore()
    for d in range(1, OWNERS):
        t = (y + d // SIDE) % SIDE * SIDE + (z + d % SIDE) % SIDE
        pl.semaphore_signal(barrier, inc=1, device_id={"owner": t}, device_id_type=MESH)
    for d in range(1, SUFS):
        t = (lane_f + d) % SUFS
        pl.semaphore_signal(barrier, inc=1, device_id={"suf": t}, device_id_type=MESH)

    pairs = (
        (q_hbm, q_v), (nk_hbm, nk_v), (nv_hbm, nv_v), (ks_hbm, ks_v), (vs_hbm, vs_v),
        (v_hbm, v_v), (k_hbm, k_v), (w_hbm, w_v),
    )
    loads = [
        pltpu.make_async_copy(src, dst, load_sem.at[i]) for i, (src, dst) in enumerate(pairs)
    ]
    for copy in loads:
        copy.start()
    ld_q, ld_nk, ld_nv, ld_ks, ld_vs, ld_v, ld_k, ld_w = loads

    lane = lax.broadcasted_iota(jnp.int32, (8, 128), 1)
    sub = lax.broadcasted_iota(jnp.int32, (8, 128), 0)
    lane_prompt, lane_place = lane // CAP, lane % CAP
    count = jnp.zeros((8, 128), jnp.int32)
    row_of = jnp.zeros((8, 128), jnp.int32)
    own_prompt = jnp.zeros((8, 128), jnp.int32)
    for r in range(ROWS):
        named = prompt_s[r]
        match = lane_prompt == named
        row_of = jnp.where(match & (count == lane_place), r, row_of)
        count = count + jnp.where(match, 1, 0)
        own_prompt = jnp.where(lane == r, named, own_prompt)
    rank = jnp.zeros((8, 128), jnp.int32)
    for r in range(ROWS):
        rank = rank + jnp.where((own_prompt == prompt_s[r]) & (lane > r), 1, 0)
    table_v[...] = jnp.where(sub == 0, row_of, rank % CAP)
    to_smem = pltpu.make_async_copy(table_v, table_s, table_sem)
    to_smem.start()
    to_smem.wait()
    ld_q.wait()

    def pack(i, carry):
        for u in range(8):
            slot = i * 8 + u
            pack_v[pl.ds(pl.multiple_of(slot * SLOT, SLOT), SLOT), :] = q_v[table_s[0, slot]]
        return carry

    lax.fori_loop(0, OWNERS * CAP // 8, pack, 0)

    def block_of(i):
        return pl.ds(pl.multiple_of(i * BLOCK, BLOCK), BLOCK)

    pl.semaphore_wait(barrier, OWNERS - 1 + SUFS - 1)

    def query_copy(t, source):
        return pltpu.make_async_remote_copy(
            src_ref=pack_v.at[block_of(t)], dst_ref=rq_v.at[block_of(source)],
            send_sem=qsend.at[t], recv_sem=qrecv.at[source],
            device_id={"owner": t}, device_id_type=MESH,
        )

    others = []
    for d in range(1, OWNERS):
        others.append((y + d // SIDE) % SIDE * SIDE + (z + d % SIDE) % SIDE)
    for t in others:
        query_copy(t, me).start()
    rq_v[block_of(me), :] = pack_v[block_of(me), :]

    ld_nk.wait()
    ld_nv.wait()
    e_v[...] = dot_t(q_v[...].reshape(ROWS * SLOT, HD), nk_v[...])
    ld_ks.wait()
    ld_vs.wait()
    slot_row = lax.broadcasted_iota(jnp.int32, (SLOT, SUFFIX), 0)
    slot_lane = lax.broadcasted_iota(jnp.int32, (SLOT, SUFFIX), 1)
    extra_row = lax.broadcasted_iota(jnp.int32, (SLOT, 2 * ROWS), 0)
    extra_lane = lax.broadcasted_iota(jnp.int32, (SLOT, 2 * ROWS), 1)

    def local_row(r):
        parent = partner_s[r] % ROWS
        rows = pl.ds(pl.multiple_of(r * SLOT, SLOT), SLOT)
        query = q_v[r]
        first = dot_t(query, ks_v[r])
        second = dot_t(query, ks_v[parent])
        scores = jnp.concatenate([first[:GROUP], second[GROUP:]], axis=0)
        used = jnp.where(slot_row < GROUP, length_s[r], length_s[parent])
        valid = slot_lane < used
        scores = jnp.where(valid, scores, -1e30)
        extra = e_v[rows, :]
        one = jnp.where(extra_row < GROUP, 2 * r, 2 * parent)
        two = jnp.where(extra_row < GROUP, 2 * r, 2 * r + 1)
        extra_valid = (extra_lane == one) | (extra_lane == two)
        extra = jnp.where(extra_valid, extra, -1e30)
        top = jnp.maximum(
            jnp.max(scores, axis=1, keepdims=True), jnp.max(extra, axis=1, keepdims=True)
        )
        weights = jnp.where(valid, jnp.exp2((scores - top) * RATE), 0.0)
        extra = jnp.where(extra_valid, jnp.exp2((extra - top) * RATE), 0.0)
        total = jnp.sum(weights, axis=1, keepdims=True) + jnp.sum(extra, axis=1, keepdims=True)
        weights = weights.astype(BF16)
        first = jnp.dot(weights, vs_v[r], preferred_element_type=F32)
        second = jnp.dot(weights, vs_v[parent], preferred_element_type=F32)
        lo_v[rows, :] = jnp.concatenate([first[:GROUP], second[GROUP:]], axis=0)
        pe_v[rows, :] = extra.astype(BF16)
        lm_v[rows, :] = jnp.broadcast_to(top, (SLOT, HD))
        ls_v[rows, :] = jnp.broadcast_to(total, (SLOT, HD))

    def local_rows(i, carry):
        for u in range(4):
            local_row(i * 4 + u)
        return carry

    lax.fori_loop(0, ROWS // 4, local_rows, 0)
    lo_v[...] += jnp.dot(pe_v[...], nv_v[...], preferred_element_type=F32)

    ld_v.wait()

    def turn(i, carry):
        at = pl.ds(pl.multiple_of(i * 512, 512), 512)
        vt_v[:, at] = v_v[at, :].T
        return carry

    lax.fori_loop(0, LENGTH // 512, turn, 0)
    ld_k.wait()
    for t in others:
        query_copy(t, t).wait_recv()

    def far(c):
        return (y + 1 + c) % SIDE

    def span_of(j):
        return pl.ds(pl.multiple_of(j * SPAN, SPAN), SPAN)

    def score(c, j):
        at = pl.ds(pl.multiple_of(far(c) * CHUNK, CHUNK), CHUNK)
        return dot_t(k_v[span_of(j), :], rq_v[at, :])

    def absorb(place, j):
        s = s_v[place]
        m_old = m_v[...]
        m_new = jnp.maximum(m_old, jnp.max(s, axis=0, keepdims=True))
        p = jnp.exp2((s - m_new[:1]) * RATE)
        decay = jnp.exp2((m_old - m_new) * RATE)
        m_v[...] = m_new
        l_v[...] = l_v[...] * decay + jnp.sum(p.reshape(SPAN // 8, 8, CHUNK), axis=0)
        acc_v[...] = acc_v[...] * decay[:1] + jnp.dot(
            vt_v[:, span_of(j)], p.astype(BF16), preferred_element_type=F32
        )

    def part_copy(t, source):
        return pltpu.make_async_remote_copy(
            src_ref=part_v.at[t], dst_ref=back_v.at[source],
            send_sem=bsend.at[t], recv_sem=brecv.at[source],
            device_id={"owner": t}, device_id_type=MESH,
        )

    def stat_copy(t, source):
        return pltpu.make_async_remote_copy(
            src_ref=stat_v.at[t], dst_ref=bstat_v.at[source],
            send_sem=ssend.at[t], recv_sem=srecv.at[source],
            device_id={"owner": t}, device_id_type=MESH,
        )

    s_v[0] = score(0, 0)

    def chunk(c, carry):
        m_v[...] = jnp.full_like(m_v, -1e30)
        l_v[...] = jnp.zeros_like(l_v)
        acc_v[...] = jnp.zeros_like(acc_v)

        def two_spans(i, inner):
            j = 2 * i
            s_v[1] = score(c, j + 1)
            absorb(0, j)
            last = jnp.where(j + 2 == SPANS, 1, 0)
            s_v[0] = score(c + last, (j + 2) % SPANS)
            absorb(1, j + 1)
            return inner

        lax.fori_loop(0, SPANS // 2, two_spans, 0)
        total = jnp.sum(l_v[...], axis=0, keepdims=True)
        top = m_v[:1, :]
        done = acc_v[...] / total
        for k in range(SIDE):
            t = far(c) * SIDE + k
            cols = slice(k * BLOCK, (k + 1) * BLOCK)
            piece = done[:, cols].T.astype(BF16)
            stats = jnp.concatenate(
                [top[:, cols], total[:, cols], jnp.zeros((6, BLOCK), F32)], axis=0
            )

            @pl.when(t == me)
            def _():
                back_v[t] = piece.reshape(CAP, SLOT, HD)
                bstat_v[t] = stats

            @pl.when(t != me)
            def _():
                part_v[t] = piece.reshape(CAP, SLOT, HD)
                stat_v[t] = stats
                part_copy(t, me).start()
                stat_copy(t, me).start()

        return carry

    lax.fori_loop(0, SIDE, chunk, 0)

    for t in others:
        part_copy(t, t).wait_recv()
        stat_copy(t, t).wait_recv()

    stats = bstat_v[...].reshape(OWNERS * 8, BLOCK)
    bstat_t[...] = stats.T.reshape(CAP, SLOT, OWNERS * 8)
    stat_lane = lax.broadcasted_iota(jnp.int32, (SLOT, OWNERS * 8), 1)

    def merge_row(r):
        named = prompt_s[r]
        rows = pl.ds(pl.multiple_of(r * SLOT, SLOT), SLOT)
        place = table_s[1, r]
        part = back_v[named, place].astype(F32)
        both = bstat_t[place]
        p_max = jnp.sum(jnp.where(stat_lane == named * 8, both, 0.0), axis=1, keepdims=True)
        p_sum = jnp.sum(jnp.where(stat_lane == named * 8 + 1, both, 0.0), axis=1, keepdims=True)
        l_max, l_sum = lm_v[rows, :], ls_v[rows, :]
        top = jnp.maximum(p_max, l_max)
        a = p_sum * jnp.exp2((p_max - top) * RATE)
        b = jnp.exp2((l_max - top) * RATE)
        merged = (a * part + b * lo_v[rows, :]) / (a + b * l_sum)
        for s in range(STEPS):
            at = pl.ds(STEPS * r + s, GROUP, stride=STEPS * ROWS)
            att_v[at, :] = merged[s * GROUP:(s + 1) * GROUP]

    for r in range(ROWS):
        merge_row(r)
    ag_v[lane_f] = att_v[...].astype(BF16)

    def gather_copy(block, to, i):
        return pltpu.make_async_remote_copy(
            src_ref=ag_v.at[block], dst_ref=ag_v.at[block],
            send_sem=gsend.at[i], recv_sem=grecv.at[block],
            device_id={"suf": to}, device_id_type=MESH,
        )

    sibling = x * 2 + 1 - core
    same = [(x + d) % SIDE * 2 + core for d in (1, 3, 2)]
    cross = [(x + d) % SIDE * 2 + 1 - core for d in (1, 3, 2)]
    sent = []
    for i, to in enumerate(same + [sibling]):
        copy = gather_copy(lane_f, to, i)
        copy.start()
        sent.append(copy)

    ld_w.wait()

    def project(block, first=False):
        a = ag_v[block]
        a = jnp.concatenate(
            [a[h * STEPS * ROWS:(h + 1) * STEPS * ROWS] for h in range(GROUP)], axis=1
        )
        w = w_v[pl.ds(pl.multiple_of(block * WIDTH, WIDTH), WIDTH), :]
        term = jnp.dot(a, w, preferred_element_type=F32)
        if first:
            proj_v[...] = term
        else:
            proj_v[...] += term

    def arrive(block):
        gather_copy(block, sibling, 0).wait_recv()

    def forward(i):
        arrive(same[i])
        copy = gather_copy(same[i], sibling, SIDE + i)
        copy.start()
        sent.append(copy)

    project(lane_f, True)
    arrive(sibling)
    project(sibling)
    forward(0)
    forward(1)
    project(same[0])
    project(same[1])
    forward(2)
    project(same[2])
    for i in range(3):
        arrive(cross[i])
        project(cross[i])
    out_ref[...] = proj_v[...].astype(BF16)

    for copy in sent:
        copy.wait_send()
    for t in others:
        query_copy(t, me).wait_send()
        part_copy(t, me).wait_send()
        stat_copy(t, me).wait_send()


def body(
    queries, new_keys, new_values, prompt_keys, prompt_values, suffix_keys, suffix_values,
    suffix_len, prompt_of_row, partner, out_weight,
):
    smem = pl.BlockSpec(memory_space=pltpu.SMEM)
    anywhere = pl.BlockSpec(memory_space=pl.ANY)
    vm = pltpu.VMEM
    dma = pltpu.SemaphoreType.DMA
    rows = STEPS * ROWS
    projected = pl.pallas_call(
        kernel,
        out_shape=jax.ShapeDtypeStruct((rows, WIDTH), BF16),
        in_specs=[smem] * 3 + [anywhere] * 8,
        out_specs=pl.BlockSpec(memory_space=pltpu.VMEM),
        scratch_shapes=[
            vm((ROWS, SLOT, HD), BF16), vm((rows, HD), BF16), vm((rows, HD), BF16),
            vm((ROWS, SUFFIX, HD), BF16), vm((ROWS, SUFFIX, HD), BF16),
            vm((LENGTH, HD), BF16), vm((LENGTH, HD), BF16), vm((HD, LENGTH), BF16),
            vm((SUFS * WIDTH, WIDTH), BF16),
            vm((8, 128), jnp.int32), pltpu.SMEM((8, 128), jnp.int32),
            vm((OWNERS * BLOCK, HD), BF16), vm((OWNERS * BLOCK, HD), BF16),
            vm((2, SPAN, CHUNK), F32), vm((8, CHUNK), F32), vm((8, CHUNK), F32), vm((HD, CHUNK), F32),
            vm((OWNERS, CAP, SLOT, HD), BF16), vm((OWNERS, 8, BLOCK), F32),
            vm((OWNERS, CAP, SLOT, HD), BF16), vm((OWNERS, 8, BLOCK), F32),
            vm((CAP, SLOT, OWNERS * 8), F32),
            vm((ROWS * SLOT, rows), F32), vm((ROWS * SLOT, rows), BF16),
            vm((ROWS * SLOT, HD), F32), vm((ROWS * SLOT, HD), F32), vm((ROWS * SLOT, HD), F32),
            vm((ROWS * SLOT, HD), F32), vm((SUFS, ROWS * SLOT, HD), BF16), vm((rows, WIDTH), F32),
            dma((8,)), dma,
            dma((OWNERS,)), dma((OWNERS,)), dma((OWNERS,)), dma((OWNERS,)),
            dma((OWNERS,)), dma((OWNERS,)), dma((SUFS,)), dma((SUFS,)),
        ],
        compiler_params=pltpu.CompilerParams(
            collective_id=0, has_side_effects=True, vmem_limit_bytes=58 * 2**20
        ),
    )(
        prompt_of_row, partner, suffix_len,
        queries.reshape(ROWS, SLOT, HD), new_keys.reshape(rows, HD), new_values.reshape(rows, HD),
        suffix_keys, suffix_values,
        prompt_keys.reshape(LENGTH, HD), prompt_values.reshape(LENGTH, HD), out_weight,
    )
    return projected.reshape(ROWS, STEPS, WIDTH)


def solution(mesh):
    return jax.shard_map(
        body,
        mesh=mesh,
        in_specs=(
            P("owner", None, "suf"),
            P("owner", None, "suf"),
            P("owner", None, "suf"),
            P("owner", "suf", None, None),
            P("owner", "suf", None, None),
            P("owner", None, "suf"),
            P("owner", None, "suf"),
            P("owner"),
            P("owner"),
            P("owner"),
            P(None, "suf"),
        ),
        out_specs=P("owner", None, "suf"),
        check_vma=False,
    )
```

```python
import jax
import jax.numpy as jnp
from jax import lax
from jax.experimental import pallas as pl
from jax.experimental.pallas import tpu as pltpu
from jax.sharding import PartitionSpec as P

MESH = pl.DeviceIdType.MESH
HD = 128
GROUP = 8
CAP = 8
STEPS = 2
SIDE = 4
OWNERS = 16
SUFS = 8
ROWS = 32
SLOT = STEPS * GROUP
BLOCK = CAP * SLOT
LENGTH = 8192
SUFFIX = 256
WIDTH = GROUP * HD
SPAN = 1024
CHUNK = SIDE * BLOCK
SPANS = LENGTH // SPAN
HALF = GROUP // 2
RATE = HD ** (-0.5) * 1.4426950408889634
F32 = jnp.float32
BF16 = jnp.bfloat16


def dot_t(a, b):
    return lax.dot_general(a, b, (((1,), (1,)), ((), ())), preferred_element_type=F32)


STEPS_Y = (0, 0, 2, 2, 1, 1, 3, 3, 2, 2, 1, 3, 0, 0, 1, 3)
STEPS_Z = (0, 2, 0, 2, 1, 3, 1, 3, 1, 3, 2, 2, 1, 3, 0, 0)
OPPOSITE = (0, 1, 2, 3, 7, 6, 5, 4, 9, 8, 11, 10, 13, 12, 15, 14)


def kernel(
    prompt_s, partner_s, length_s,
    q_hbm, nk_hbm, nv_hbm, ks_hbm, vs_hbm, k_hbm, v_hbm, w_hbm,
    out_ref,
    q_v, nk_v, nv_v, ks_v, vs_v, k_v, v_v, vt_v, w_v,
    table_v, table_s, pack_v, rq_v,
    s_v, p_v, top_v, m_v, l_v, acc_v,
    part_v, stat_v, back_v, bstat_v, bstat_t,
    e_v, pe_v, lo_v, lm_v, ls_v,
    att_v, ag_v, proj_v,
    load_sem, table_sem,
    qsend, qrecv, bsend, brecv, ssend, srecv, gsend, grecv,
):
    me = lax.axis_index("owner")
    mine = lax.axis_index("suf")
    y, z = me // SIDE, me % SIDE
    x, core = mine // 2, mine % 2
    right, left = (x + 1) % SIDE * 2 + core, (x + 3) % SIDE * 2 + core
    across = (x + 2) % SIDE * 2 + core
    sibling = x * 2 + 1 - core

    def owner_at(dy, dz):
        return (y + dy) % SIDE * SIDE + (z + dz) % SIDE

    others = [(i, owner_at(STEPS_Y[i], STEPS_Z[i])) for i in range(1, OWNERS)]

    barrier = pltpu.get_barrier_semaphore()
    for _, t in others:
        pl.semaphore_signal(barrier, inc=1, device_id={"owner": t}, device_id_type=MESH)
    for t in (right, left, sibling):
        pl.semaphore_signal(barrier, inc=1, device_id={"suf": t}, device_id_type=MESH)

    pairs = (
        (q_hbm, q_v), (nk_hbm, nk_v), (nv_hbm, nv_v), (ks_hbm, ks_v), (vs_hbm, vs_v),
        (v_hbm, v_v), (k_hbm, k_v), (w_hbm, w_v),
    )
    loads = [
        pltpu.make_async_copy(src, dst, load_sem.at[i]) for i, (src, dst) in enumerate(pairs)
    ]
    for copy in loads:
        copy.start()
    ld_q, ld_nk, ld_nv, ld_ks, ld_vs, ld_v, ld_k, ld_w = loads

    lane = lax.broadcasted_iota(jnp.int32, (8, 128), 1)
    sub = lax.broadcasted_iota(jnp.int32, (8, 128), 0)
    lane_prompt, lane_place = lane // CAP, lane % CAP
    count = jnp.zeros((8, 128), jnp.int32)
    row_of = jnp.zeros((8, 128), jnp.int32)
    own_prompt = jnp.zeros((8, 128), jnp.int32)
    for r in range(ROWS):
        named = prompt_s[r]
        match = lane_prompt == named
        row_of = jnp.where(match & (count == lane_place), r, row_of)
        count = count + jnp.where(match, 1, 0)
        own_prompt = jnp.where(lane == r, named, own_prompt)
    rank = jnp.zeros((8, 128), jnp.int32)
    for r in range(ROWS):
        rank = rank + jnp.where((own_prompt == prompt_s[r]) & (lane > r), 1, 0)
    table_v[...] = jnp.where(sub == 0, row_of, rank % CAP)
    to_smem = pltpu.make_async_copy(table_v, table_s, table_sem)
    to_smem.start()
    to_smem.wait()
    ld_q.wait()

    def pack(i, carry):
        for u in range(8):
            slot = i * 8 + u
            pack_v[pl.ds(pl.multiple_of(slot * SLOT, SLOT), SLOT), :] = q_v[table_s[0, slot]]
        return carry

    lax.fori_loop(0, OWNERS * CAP // 8, pack, 0)

    def block_of(i):
        return pl.ds(pl.multiple_of(i * BLOCK, BLOCK), BLOCK)

    pl.semaphore_wait(barrier, OWNERS - 1 + 3)

    def query_copy(t, i, there):
        return pltpu.make_async_remote_copy(
            src_ref=pack_v.at[block_of(t)], dst_ref=rq_v.at[block_of(there)],
            send_sem=qsend.at[i], recv_sem=qrecv.at[there],
            device_id={"owner": t}, device_id_type=MESH,
        )

    for i, t in others:
        query_copy(t, i, OPPOSITE[i]).start()
    rq_v[block_of(0), :] = pack_v[block_of(me), :]

    ld_nk.wait()
    ld_nv.wait()
    e_v[...] = dot_t(q_v[...].reshape(ROWS * SLOT, HD), nk_v[...])
    ld_ks.wait()
    ld_vs.wait()
    early = lax.broadcasted_iota(jnp.int32, (SLOT, SUFFIX), 0) % STEPS == 0
    slot_lane = lax.broadcasted_iota(jnp.int32, (SLOT, SUFFIX), 1)
    extra_early = lax.broadcasted_iota(jnp.int32, (SLOT, 2 * ROWS), 0) % STEPS == 0
    extra_lane = lax.broadcasted_iota(jnp.int32, (SLOT, 2 * ROWS), 1)
    part_early = lax.broadcasted_iota(jnp.int32, (SLOT, HD), 0) % STEPS == 0

    def local_row(r):
        parent = partner_s[r] % ROWS
        rows = pl.ds(pl.multiple_of(r * SLOT, SLOT), SLOT)
        query = q_v[r]
        scores = jnp.where(early, dot_t(query, ks_v[r]), dot_t(query, ks_v[parent]))
        valid = slot_lane < jnp.where(early, length_s[r], length_s[parent])
        scores = jnp.where(valid, scores, -1e30)
        extra = e_v[rows, :]
        one = jnp.where(extra_early, 2 * r, 2 * parent)
        two = jnp.where(extra_early, 2 * r, 2 * r + 1)
        extra_valid = (extra_lane == one) | (extra_lane == two)
        extra = jnp.where(extra_valid, extra, -1e30)
        top = jnp.maximum(
            jnp.max(scores, axis=1, keepdims=True), jnp.max(extra, axis=1, keepdims=True)
        )
        weights = jnp.where(valid, jnp.exp2((scores - top) * RATE), 0.0)
        extra = jnp.where(extra_valid, jnp.exp2((extra - top) * RATE), 0.0)
        total = jnp.sum(weights, axis=1, keepdims=True) + jnp.sum(extra, axis=1, keepdims=True)
        weights = weights.astype(BF16)
        first = jnp.dot(weights, vs_v[r], preferred_element_type=F32)
        second = jnp.dot(weights, vs_v[parent], preferred_element_type=F32)
        lo_v[rows, :] = jnp.where(part_early, first, second)
        pe_v[rows, :] = extra.astype(BF16)
        lm_v[rows, :] = jnp.broadcast_to(top, (SLOT, HD))
        ls_v[rows, :] = jnp.broadcast_to(total, (SLOT, HD))

    def local_rows(i, carry):
        for u in range(4):
            local_row(i * 4 + u)
        return carry

    lax.fori_loop(0, ROWS // 4, local_rows, 0)
    lo_v[...] += jnp.dot(pe_v[...], nv_v[...], preferred_element_type=F32)

    ld_v.wait()

    def turn(i, carry):
        at = pl.ds(pl.multiple_of(i * 512, 512), 512)
        vt_v[:, at] = v_v[at, :].T
        return carry

    lax.fori_loop(0, LENGTH // 512, turn, 0)
    ld_k.wait()
    for i in range(1, 2 * SIDE):
        query_copy(others[0][1], i, i).wait_recv()

    def score(c, j):
        at = pl.ds(pl.multiple_of(c * CHUNK, CHUNK), CHUNK)
        s = dot_t(k_v[j * SPAN:(j + 1) * SPAN, :], rq_v[at, :])
        s_v[j % 2] = s
        top_v[j % 2] = jnp.max(s.reshape(SPAN // 8, 8, CHUNK), axis=0)

    def absorb(j):
        top = jnp.max(top_v[j % 2], axis=0, keepdims=True)
        if j == 0:
            m_new = jnp.broadcast_to(top, (8, CHUNK))
        else:
            m_old = m_v[...]
            m_new = jnp.maximum(m_old, top)
            decay = jnp.exp2((m_old - m_new) * RATE)
        m_v[...] = m_new
        p = jnp.exp2((s_v[j % 2] - m_new[:1]) * RATE)
        total = jnp.sum(p.reshape(SPAN // 8, 8, CHUNK), axis=0)
        p_v[...] = p.astype(BF16)
        term = jnp.dot(
            vt_v[:, j * SPAN:(j + 1) * SPAN], p_v[...], preferred_element_type=F32
        )
        if j == 0:
            l_v[...] = total
            acc_v[...] = term
        else:
            l_v[...] = l_v[...] * decay + total
            acc_v[...] = acc_v[...] * decay[:1] + term

    def part_copy(i, t, source):
        return pltpu.make_async_remote_copy(
            src_ref=part_v.at[i], dst_ref=back_v.at[source],
            send_sem=bsend.at[i], recv_sem=brecv.at[source],
            device_id={"owner": t}, device_id_type=MESH,
        )

    def stat_copy(i, t, source):
        return pltpu.make_async_remote_copy(
            src_ref=stat_v.at[i], dst_ref=bstat_v.at[source],
            send_sem=ssend.at[i], recv_sem=srecv.at[source],
            device_id={"owner": t}, device_id_type=MESH,
        )

    def pick(table, c, k):
        value = table[k]
        for n in range(1, SIDE):
            value = jnp.where(c == n, table[n * SIDE + k], value)
        return value

    score(0, 0)

    def chunk(c, carry):
        @pl.when((c > 0) & (c < SIDE - 1))
        def _():
            for k in range(SIDE):
                query_copy(others[0][1], (c + 1) * SIDE + k, (c + 1) * SIDE + k).wait_recv()

        for j in range(SPANS):
            if j + 1 < SPANS:
                score(c, j + 1)
            else:
                score(jnp.minimum(c + 1, SIDE - 1), 0)
            absorb(j)
        total = jnp.sum(l_v[...], axis=0, keepdims=True)
        top = m_v[:1, :]
        done = acc_v[...] / total
        for k in range(SIDE):
            i = c * SIDE + k
            t = owner_at(pick(STEPS_Y, c, k), pick(STEPS_Z, c, k))
            cols = slice(k * BLOCK, (k + 1) * BLOCK)
            piece = done[:, cols].T.astype(BF16).reshape(CAP, SLOT, HD)
            stats = jnp.concatenate(
                [top[:, cols], total[:, cols], jnp.zeros((6, BLOCK), F32)], axis=0
            )

            @pl.when(i == 0)
            def _():
                back_v[me] = piece
                bstat_v[me] = stats

            @pl.when(i != 0)
            def _():
                part_v[i] = piece
                stat_v[i] = stats
                part_copy(i, t, me).start()
                stat_copy(i, t, me).start()

        return carry

    lax.fori_loop(0, SIDE, chunk, 0)

    for i, t in others:
        part_copy(i, t, t).wait_recv()
        stat_copy(i, t, t).wait_recv()

    bstat_t[...] = bstat_v[...].reshape(OWNERS * 8, BLOCK).T.reshape(CAP, SLOT, OWNERS * 8)
    stat_lane = lax.broadcasted_iota(jnp.int32, (SLOT, OWNERS * 8), 1)

    def merge_row(r):
        named = prompt_s[r]
        rows = pl.ds(pl.multiple_of(r * SLOT, SLOT), SLOT)
        place = table_s[1, r]
        part = back_v[named, place].astype(F32)
        both = bstat_t[place]
        p_max = jnp.sum(jnp.where(stat_lane == named * 8, both, 0.0), axis=1, keepdims=True)
        p_sum = jnp.sum(jnp.where(stat_lane == named * 8 + 1, both, 0.0), axis=1, keepdims=True)
        l_max, l_sum = lm_v[rows, :], ls_v[rows, :]
        top = jnp.maximum(p_max, l_max)
        a = p_sum * jnp.exp2((p_max - top) * RATE)
        b = jnp.exp2((l_max - top) * RATE)
        att_v[rows, :] = (a * part + b * lo_v[rows, :]) / (a + b * l_sum)

    for r in range(ROWS):
        merge_row(r)
    for h in range(GROUP):
        both = [att_v[pl.ds(STEPS * h + s, ROWS, stride=SLOT), :] for s in range(STEPS)]
        ag_v[mine, h // HALF, h % HALF] = jnp.concatenate(both, axis=0).astype(BF16)

    sent = []

    def gather_copy(block, half, to, i):
        return pltpu.make_async_remote_copy(
            src_ref=ag_v.at[block, half], dst_ref=ag_v.at[block, half],
            send_sem=gsend.at[i], recv_sem=grecv.at[block, half],
            device_id={"suf": to}, device_id_type=MESH,
        )

    def send(block, half, to):
        copy = gather_copy(block, half, to, len(sent))
        copy.start()
        sent.append(copy)

    def arrive(block, half):
        gather_copy(block, half, sibling, 0).wait_recv()

    def project(block, half, first=False):
        a = ag_v[block, half]
        a = jnp.concatenate([a[h] for h in range(HALF)], axis=1)
        start = block * WIDTH + half * HALF * HD
        w = w_v[pl.ds(pl.multiple_of(start, HALF * HD), HALF * HD), :]
        term = jnp.dot(a, w, preferred_element_type=F32)
        if first:
            proj_v[...] = term
        else:
            proj_v[...] += term

    send(mine, 0, right)
    send(mine, 1, left)
    send(mine, 1, right)
    send(mine, 0, left)
    send(mine, 0, sibling)
    send(mine, 1, sibling)
    ld_w.wait()
    project(mine, 0, True)
    project(mine, 1)
    arrive(left, 0)
    send(left, 0, right)
    send(left, 0, sibling)
    arrive(right, 1)
    send(right, 1, left)
    send(right, 1, sibling)
    for half in range(2):
        arrive(sibling, half)
        project(sibling, half)
    project(left, 0)
    project(right, 1)
    for block, half in ((left, 1), (right, 0)):
        arrive(block, half)
        send(block, half, sibling)
    project(left, 1)
    project(right, 0)
    for half in range(2):
        arrive(across, half)
        send(across, half, sibling)
    project(across, 0)
    project(across, 1)
    turned = 1 - 2 * core
    for block, half in (
        (left, 0), (right, 1), (left, 1), (right, 0), (across, 0), (across, 1),
    ):
        arrive(block + turned, half)
        project(block + turned, half)

    for j in range(GROUP):
        for s in range(STEPS):
            att_v[pl.ds(STEPS * j + s, ROWS, stride=SLOT), :] = (
                proj_v[s * ROWS:(s + 1) * ROWS, j * HD:(j + 1) * HD]
            )
    out_ref[...] = att_v[...].astype(BF16).reshape(ROWS, SLOT, HD)

    for copy in sent:
        copy.wait_send()
    for i, t in others:
        query_copy(t, i, OPPOSITE[i]).wait_send()
        part_copy(i, t, me).wait_send()
        stat_copy(i, t, me).wait_send()


def body(
    queries, new_keys, new_values, prompt_keys, prompt_values, suffix_keys, suffix_values,
    suffix_len, prompt_of_row, partner, out_weight,
):
    smem = pl.BlockSpec(memory_space=pltpu.SMEM)
    anywhere = pl.BlockSpec(memory_space=pl.ANY)
    vm = pltpu.VMEM
    dma = pltpu.SemaphoreType.DMA
    rows = STEPS * ROWS
    projected = pl.pallas_call(
        kernel,
        out_shape=jax.ShapeDtypeStruct((ROWS, SLOT, HD), BF16),
        in_specs=[smem] * 3 + [anywhere] * 8,
        out_specs=pl.BlockSpec(memory_space=pltpu.VMEM),
        scratch_shapes=[
            vm((ROWS, SLOT, HD), BF16), vm((rows, HD), BF16), vm((rows, HD), BF16),
            vm((ROWS, SUFFIX, HD), BF16), vm((ROWS, SUFFIX, HD), BF16),
            vm((LENGTH, HD), BF16), vm((LENGTH, HD), BF16), vm((HD, LENGTH), BF16),
            vm((SUFS * WIDTH, WIDTH), BF16),
            vm((8, 128), jnp.int32), pltpu.SMEM((8, 128), jnp.int32),
            vm((OWNERS * BLOCK, HD), BF16), vm((OWNERS * BLOCK, HD), BF16),
            vm((2, SPAN, CHUNK), F32), vm((SPAN, CHUNK), BF16), vm((2, 8, CHUNK), F32),
            vm((8, CHUNK), F32), vm((8, CHUNK), F32), vm((HD, CHUNK), F32),
            vm((OWNERS, CAP, SLOT, HD), BF16), vm((OWNERS, 8, BLOCK), F32),
            vm((OWNERS, CAP, SLOT, HD), BF16), vm((OWNERS, 8, BLOCK), F32),
            vm((CAP, SLOT, OWNERS * 8), F32),
            vm((ROWS * SLOT, rows), F32), vm((ROWS * SLOT, rows), BF16),
            vm((ROWS * SLOT, HD), F32), vm((ROWS * SLOT, HD), F32), vm((ROWS * SLOT, HD), F32),
            vm((ROWS * SLOT, HD), F32), vm((SUFS, 2, HALF, rows, HD), BF16), vm((rows, WIDTH), F32),
            dma((8,)), dma,
            dma((OWNERS,)), dma((OWNERS,)), dma((OWNERS,)), dma((OWNERS,)),
            dma((OWNERS,)), dma((OWNERS,)), dma((14,)), dma((SUFS, 2)),
        ],
        compiler_params=pltpu.CompilerParams(
            collective_id=0, has_side_effects=True, vmem_limit_bytes=58 * 2**20
        ),
    )(
        prompt_of_row, partner, suffix_len,
        queries.reshape(ROWS, STEPS, GROUP, HD).swapaxes(1, 2).reshape(ROWS, SLOT, HD), new_keys.reshape(rows, HD), new_values.reshape(rows, HD),
        suffix_keys, suffix_values,
        prompt_keys.reshape(LENGTH, HD), prompt_values.reshape(LENGTH, HD), out_weight,
    )
    projected = projected.reshape(ROWS, GROUP, STEPS, HD).swapaxes(1, 2)
    return projected.reshape(ROWS, STEPS, WIDTH)


def solution(mesh):
    return jax.shard_map(
        body,
        mesh=mesh,
        in_specs=(
            P("owner", None, "suf"),
            P("owner", None, "suf"),
            P("owner", None, "suf"),
            P("owner", "suf", None, None),
            P("owner", "suf", None, None),
            P("owner", None, "suf"),
            P("owner", None, "suf"),
            P("owner"),
            P("owner"),
            P("owner"),
            P(None, "suf"),
        ),
        out_specs=P("owner", None, "suf"),
        check_vma=False,
    )
```

```python
import jax
import jax.numpy as jnp
from jax import lax
from jax.experimental import pallas as pl
from jax.experimental.pallas import tpu as pltpu
from jax.sharding import PartitionSpec as P

MESH = pl.DeviceIdType.MESH
HD = 128
GROUP = 8
CAP = 8
STEPS = 2
SIDE = 4
OWNERS = 16
SUFS = 8
ROWS = 32
SLOT = STEPS * GROUP
BLOCK = CAP * SLOT
LENGTH = 8192
SUFFIX = 256
WIDTH = GROUP * HD
SPAN = 1024
CHUNK = SIDE * BLOCK
SPANS = LENGTH // SPAN
PIECES = 4
HEADS = GROUP // PIECES
RATE = HD ** (-0.5) * 1.4426950408889634
F32 = jnp.float32
BF16 = jnp.bfloat16


def dot_t(a, b):
    return lax.dot_general(a, b, (((1,), (1,)), ((), ())), preferred_element_type=F32)


STEPS_Y = (0, 0, 2, 2, 1, 1, 3, 3, 2, 2, 1, 3, 0, 0, 1, 3)
STEPS_Z = (0, 2, 0, 2, 1, 3, 1, 3, 1, 3, 2, 2, 1, 3, 0, 0)
OPPOSITE = (0, 1, 2, 3, 7, 6, 5, 4, 9, 8, 11, 10, 13, 12, 15, 14)


def kernel(
    prompt_s, partner_s, length_s,
    q_hbm, nk_hbm, nv_hbm, ks_hbm, vs_hbm, k_hbm, v_hbm, w_hbm,
    out_ref,
    q_v, nk_v, nv_v, ks_v, vs_v, k_v, v_v, vt_v, w_v,
    table_v, table_s, pack_v, rq_v,
    s_v, p_v, top_v, m_v, l_v, acc_v,
    part_v, stat_v, back_v, bstat_v, bstat_t,
    e_v, pe_v, ls_v, lw_v, lo_v, lm_v, lt_v,
    att_v, ag_v, proj_v,
    load_sem, table_sem,
    qsend, qrecv, bsend, brecv, ssend, srecv, gsend, grecv,
):
    me = lax.axis_index("owner")
    mine = lax.axis_index("suf")
    y, z = me // SIDE, me % SIDE
    x, core = mine // 2, mine % 2
    right, left = (x + 1) % SIDE * 2 + core, (x + 3) % SIDE * 2 + core
    across = (x + 2) % SIDE * 2 + core
    sibling = x * 2 + 1 - core

    def owner_at(dy, dz):
        return (y + dy) % SIDE * SIDE + (z + dz) % SIDE

    others = [(i, owner_at(STEPS_Y[i], STEPS_Z[i])) for i in range(1, OWNERS)]

    barrier = pltpu.get_barrier_semaphore()
    for _, t in others:
        pl.semaphore_signal(barrier, inc=1, device_id={"owner": t}, device_id_type=MESH)
    for t in (right, left, sibling):
        pl.semaphore_signal(barrier, inc=1, device_id={"suf": t}, device_id_type=MESH)

    pairs = (
        (q_hbm, q_v), (nk_hbm, nk_v), (nv_hbm, nv_v), (ks_hbm, ks_v), (vs_hbm, vs_v),
        (v_hbm, v_v), (k_hbm, k_v), (w_hbm, w_v),
    )
    loads = [
        pltpu.make_async_copy(src, dst, load_sem.at[i]) for i, (src, dst) in enumerate(pairs)
    ]
    for copy in loads:
        copy.start()
    ld_q, ld_nk, ld_nv, ld_ks, ld_vs, ld_v, ld_k, ld_w = loads

    lane = lax.broadcasted_iota(jnp.int32, (8, 128), 1)
    sub = lax.broadcasted_iota(jnp.int32, (8, 128), 0)
    lane_prompt, lane_place = lane // CAP, lane % CAP
    count = jnp.zeros((8, 128), jnp.int32)
    row_of = jnp.zeros((8, 128), jnp.int32)
    own_prompt = jnp.zeros((8, 128), jnp.int32)
    for r in range(ROWS):
        named = prompt_s[r]
        match = lane_prompt == named
        row_of = jnp.where(match & (count == lane_place), r, row_of)
        count = count + jnp.where(match, 1, 0)
        own_prompt = jnp.where(lane == r, named, own_prompt)
    rank = jnp.zeros((8, 128), jnp.int32)
    for r in range(ROWS):
        rank = rank + jnp.where((own_prompt == prompt_s[r]) & (lane > r), 1, 0)
    table_v[...] = jnp.where(sub == 0, row_of, rank % CAP)
    to_smem = pltpu.make_async_copy(table_v, table_s, table_sem)
    to_smem.start()
    to_smem.wait()
    ld_q.wait()

    def pack(i, carry):
        for u in range(8):
            slot = i * 8 + u
            pack_v[pl.ds(pl.multiple_of(slot * SLOT, SLOT), SLOT), :] = q_v[table_s[0, slot]]
        return carry

    lax.fori_loop(0, OWNERS * CAP // 8, pack, 0)

    def block_of(i):
        return pl.ds(pl.multiple_of(i * BLOCK, BLOCK), BLOCK)

    pl.semaphore_wait(barrier, OWNERS - 1 + 3)

    def query_copy(t, i, there):
        return pltpu.make_async_remote_copy(
            src_ref=pack_v.at[block_of(t)], dst_ref=rq_v.at[block_of(there)],
            send_sem=qsend.at[i], recv_sem=qrecv.at[there],
            device_id={"owner": t}, device_id_type=MESH,
        )

    for i, t in others:
        query_copy(t, i, OPPOSITE[i]).start()
    rq_v[block_of(0), :] = pack_v[block_of(me), :]

    ld_nk.wait()
    ld_nv.wait()
    e_v[...] = dot_t(q_v[...].reshape(ROWS * SLOT, HD), nk_v[...])
    ld_ks.wait()
    ld_vs.wait()
    early = lax.broadcasted_iota(jnp.int32, (SLOT, SUFFIX), 0) % STEPS == 0
    slot_lane = lax.broadcasted_iota(jnp.int32, (SLOT, SUFFIX), 1)
    extra_early = lax.broadcasted_iota(jnp.int32, (SLOT, 2 * ROWS), 0) % STEPS == 0
    extra_lane = lax.broadcasted_iota(jnp.int32, (SLOT, 2 * ROWS), 1)
    part_early = lax.broadcasted_iota(jnp.int32, (SLOT, HD), 0) % STEPS == 0

    def local_scores(r):
        parent = partner_s[r] % ROWS
        rows = pl.ds(pl.multiple_of(r * SLOT, SLOT), SLOT)
        query = q_v[r]
        scores = jnp.where(early, dot_t(query, ks_v[r]), dot_t(query, ks_v[parent]))
        valid = slot_lane < jnp.where(early, length_s[r], length_s[parent])
        ls_v[rows, :] = jnp.where(valid, scores, -1e30)
        one = jnp.where(extra_early, 2 * r, 2 * parent)
        two = jnp.where(extra_early, 2 * r, 2 * r + 1)
        extra_valid = (extra_lane == one) | (extra_lane == two)
        e_v[rows, :] = jnp.where(extra_valid, e_v[rows, :], -1e30)

    def local_weights(i):
        rows = pl.ds(pl.multiple_of(i * BLOCK, BLOCK), BLOCK)
        scores, extra = ls_v[rows, :], e_v[rows, :]
        top = jnp.maximum(
            jnp.max(scores, axis=1, keepdims=True), jnp.max(extra, axis=1, keepdims=True)
        )
        weights = jnp.exp2((scores - top) * RATE)
        extra = jnp.exp2((extra - top) * RATE)
        total = jnp.sum(weights, axis=1, keepdims=True) + jnp.sum(extra, axis=1, keepdims=True)
        lw_v[rows, :] = weights.astype(BF16)
        pe_v[rows, :] = extra.astype(BF16)
        lm_v[rows, :] = jnp.broadcast_to(top, (BLOCK, HD))
        lt_v[rows, :] = jnp.broadcast_to(total, (BLOCK, HD))

    def local_values(r):
        parent = partner_s[r] % ROWS
        rows = pl.ds(pl.multiple_of(r * SLOT, SLOT), SLOT)
        weights = lw_v[rows, :]
        first = jnp.dot(weights, vs_v[r], preferred_element_type=F32)
        second = jnp.dot(weights, vs_v[parent], preferred_element_type=F32)
        lo_v[rows, :] = jnp.where(part_early, first, second)

    def by_eight(step):
        def run(i, carry):
            for u in range(8):
                step(i * 8 + u)
            return carry

        lax.fori_loop(0, ROWS // 8, run, 0)

    by_eight(local_scores)
    for i in range(ROWS * SLOT // BLOCK):
        local_weights(i)
    by_eight(local_values)
    lo_v[...] += jnp.dot(pe_v[...], nv_v[...], preferred_element_type=F32)

    ld_v.wait()

    def turn(i, carry):
        at = pl.ds(pl.multiple_of(i * 512, 512), 512)
        vt_v[:, at] = v_v[at, :].T
        return carry

    lax.fori_loop(0, LENGTH // 512, turn, 0)
    ld_k.wait()
    for i in range(1, 2 * SIDE):
        query_copy(others[0][1], i, i).wait_recv()

    def score(c, j):
        at = pl.ds(pl.multiple_of(c * CHUNK, CHUNK), CHUNK)
        s = dot_t(k_v[j * SPAN:(j + 1) * SPAN, :], rq_v[at, :])
        s_v[j % 2] = s
        top_v[j % 2] = jnp.max(s.reshape(SPAN // 8, 8, CHUNK), axis=0)

    def absorb(j):
        top = jnp.max(top_v[j % 2], axis=0, keepdims=True)
        if j == 0:
            m_new = jnp.broadcast_to(top, (8, CHUNK))
        else:
            m_old = m_v[...]
            m_new = jnp.maximum(m_old, top)
            decay = jnp.exp2((m_old - m_new) * RATE)
        m_v[...] = m_new
        p = jnp.exp2((s_v[j % 2] - m_new[:1]) * RATE)
        total = jnp.sum(p.reshape(SPAN // 8, 8, CHUNK), axis=0)
        p_v[...] = p.astype(BF16)
        term = jnp.dot(
            vt_v[:, j * SPAN:(j + 1) * SPAN], p_v[...], preferred_element_type=F32
        )
        if j == 0:
            l_v[...] = total
            acc_v[...] = term
        else:
            l_v[...] = l_v[...] * decay + total
            acc_v[...] = acc_v[...] * decay[:1] + term

    def part_copy(i, t, source):
        return pltpu.make_async_remote_copy(
            src_ref=part_v.at[i], dst_ref=back_v.at[source],
            send_sem=bsend.at[i], recv_sem=brecv.at[source],
            device_id={"owner": t}, device_id_type=MESH,
        )

    def stat_copy(i, t, source):
        return pltpu.make_async_remote_copy(
            src_ref=stat_v.at[i], dst_ref=bstat_v.at[source],
            send_sem=ssend.at[i], recv_sem=srecv.at[source],
            device_id={"owner": t}, device_id_type=MESH,
        )

    def pick(table, c, k):
        value = table[k]
        for n in range(1, SIDE):
            value = jnp.where(c == n, table[n * SIDE + k], value)
        return value

    score(0, 0)

    def chunk(c, carry):
        @pl.when((c > 0) & (c < SIDE - 1))
        def _():
            for k in range(SIDE):
                query_copy(others[0][1], (c + 1) * SIDE + k, (c + 1) * SIDE + k).wait_recv()

        for j in range(SPANS):
            if j + 1 < SPANS:
                score(c, j + 1)
            else:
                score(jnp.minimum(c + 1, SIDE - 1), 0)
            absorb(j)
        total = jnp.sum(l_v[...], axis=0, keepdims=True)
        top = m_v[:1, :]
        done = acc_v[...] / total
        for k in range(SIDE):
            i = c * SIDE + k
            t = owner_at(pick(STEPS_Y, c, k), pick(STEPS_Z, c, k))
            cols = slice(k * BLOCK, (k + 1) * BLOCK)
            piece = done[:, cols].T.astype(BF16).reshape(CAP, SLOT, HD)
            stats = jnp.concatenate(
                [top[:, cols], total[:, cols], jnp.zeros((6, BLOCK), F32)], axis=0
            )

            @pl.when(i == 0)
            def _():
                back_v[me] = piece
                bstat_v[me] = stats

            @pl.when(i != 0)
            def _():
                part_v[i] = piece
                stat_v[i] = stats
                part_copy(i, t, me).start()
                stat_copy(i, t, me).start()

        return carry

    lax.fori_loop(0, SIDE, chunk, 0)

    for i, t in others:
        part_copy(i, t, t).wait_recv()
        stat_copy(i, t, t).wait_recv()

    bstat_t[...] = bstat_v[...].reshape(OWNERS * 8, BLOCK).T.reshape(CAP, SLOT, OWNERS * 8)
    stat_lane = lax.broadcasted_iota(jnp.int32, (SLOT, OWNERS * 8), 1)

    def merge_row(r):
        named = prompt_s[r]
        rows = pl.ds(pl.multiple_of(r * SLOT, SLOT), SLOT)
        place = table_s[1, r]
        part = back_v[named, place].astype(F32)
        both = bstat_t[place]
        p_max = jnp.sum(jnp.where(stat_lane == named * 8, both, 0.0), axis=1, keepdims=True)
        p_sum = jnp.sum(jnp.where(stat_lane == named * 8 + 1, both, 0.0), axis=1, keepdims=True)
        l_max, l_sum = lm_v[rows, :], lt_v[rows, :]
        top = jnp.maximum(p_max, l_max)
        a = p_sum * jnp.exp2((p_max - top) * RATE)
        b = jnp.exp2((l_max - top) * RATE)
        att_v[rows, :] = (a * part + b * lo_v[rows, :]) / (a + b * l_sum)

    for r in range(ROWS):
        merge_row(r)
    sent = []

    def gather_copy(block, piece, to, i):
        return pltpu.make_async_remote_copy(
            src_ref=ag_v.at[block, piece], dst_ref=ag_v.at[block, piece],
            send_sem=gsend.at[i], recv_sem=grecv.at[block, piece],
            device_id={"suf": to}, device_id_type=MESH,
        )

    def send(block, piece, to):
        copy = gather_copy(block, piece, to, len(sent))
        copy.start()
        sent.append(copy)

    def arrive(block, piece):
        gather_copy(block, piece, sibling, 0).wait_recv()

    def project(block, piece, first=False):
        a = ag_v[block, piece]
        a = jnp.concatenate([a[h] for h in range(HEADS)], axis=1)
        start = block * WIDTH + piece * HEADS * HD
        w = w_v[pl.ds(pl.multiple_of(start, HEADS * HD), HEADS * HD), :]
        term = jnp.dot(a, w, preferred_element_type=F32)
        if first:
            proj_v[...] = term
        else:
            proj_v[...] += term

    def ready(piece):
        for h in range(piece * HEADS, (piece + 1) * HEADS):
            both = [att_v[pl.ds(STEPS * h + s, ROWS, stride=SLOT), :] for s in range(STEPS)]
            ag_v[mine, piece, h % HEADS] = jnp.concatenate(both, axis=0).astype(BF16)

    middle = PIECES // 2
    for p in range(middle):
        ready(p)
        send(mine, p, right)
        ready(middle + p)
        send(mine, middle + p, left)
    for p in range(middle):
        send(mine, middle + p, right)
        send(mine, p, left)
    for p in range(PIECES):
        send(mine, p, sibling)
    ld_w.wait()
    for p in range(PIECES):
        project(mine, p, p == 0)
    for p in range(middle):
        arrive(left, p)
        send(left, p, right)
        send(left, p, sibling)
        arrive(right, middle + p)
        send(right, middle + p, left)
        send(right, middle + p, sibling)
    for p in range(PIECES):
        arrive(sibling, p)
        project(sibling, p)
    for p in range(middle):
        project(left, p)
        project(right, middle + p)
    for p in range(middle):
        arrive(left, middle + p)
        send(left, middle + p, sibling)
        arrive(right, p)
        send(right, p, sibling)
    for p in range(middle):
        project(left, middle + p)
        project(right, p)
    for p in range(middle):
        arrive(across, p)
        send(across, p, sibling)
        arrive(across, middle + p)
        send(across, middle + p, sibling)
    for p in range(PIECES):
        project(across, p)
    turned = 1 - 2 * core
    for p in range(middle):
        for block, piece in ((left, p), (right, middle + p)):
            arrive(block + turned, piece)
            project(block + turned, piece)
    for p in range(middle):
        for block, piece in ((left, middle + p), (right, p)):
            arrive(block + turned, piece)
            project(block + turned, piece)
    for p in range(middle):
        for piece in (p, middle + p):
            arrive(across + turned, piece)
            project(across + turned, piece)

    for j in range(GROUP):
        for s in range(STEPS):
            att_v[pl.ds(STEPS * j + s, ROWS, stride=SLOT), :] = (
                proj_v[s * ROWS:(s + 1) * ROWS, j * HD:(j + 1) * HD]
            )
    out_ref[...] = att_v[...].astype(BF16).reshape(ROWS, SLOT, HD)

    for copy in sent:
        copy.wait_send()
    for i, t in others:
        query_copy(t, i, OPPOSITE[i]).wait_send()
        part_copy(i, t, me).wait_send()
        stat_copy(i, t, me).wait_send()


def body(
    queries, new_keys, new_values, prompt_keys, prompt_values, suffix_keys, suffix_values,
    suffix_len, prompt_of_row, partner, out_weight,
):
    smem = pl.BlockSpec(memory_space=pltpu.SMEM)
    anywhere = pl.BlockSpec(memory_space=pl.ANY)
    vm = pltpu.VMEM
    dma = pltpu.SemaphoreType.DMA
    rows = STEPS * ROWS
    projected = pl.pallas_call(
        kernel,
        out_shape=jax.ShapeDtypeStruct((ROWS, SLOT, HD), BF16),
        in_specs=[smem] * 3 + [anywhere] * 8,
        out_specs=pl.BlockSpec(memory_space=pltpu.VMEM),
        scratch_shapes=[
            vm((ROWS, SLOT, HD), BF16), vm((rows, HD), BF16), vm((rows, HD), BF16),
            vm((ROWS, SUFFIX, HD), BF16), vm((ROWS, SUFFIX, HD), BF16),
            vm((LENGTH, HD), BF16), vm((LENGTH, HD), BF16), vm((HD, LENGTH), BF16),
            vm((SUFS * WIDTH, WIDTH), BF16),
            vm((8, 128), jnp.int32), pltpu.SMEM((8, 128), jnp.int32),
            vm((OWNERS * BLOCK, HD), BF16), vm((OWNERS * BLOCK, HD), BF16),
            vm((2, SPAN, CHUNK), F32), vm((SPAN, CHUNK), BF16), vm((2, 8, CHUNK), F32),
            vm((8, CHUNK), F32), vm((8, CHUNK), F32), vm((HD, CHUNK), F32),
            vm((OWNERS, CAP, SLOT, HD), BF16), vm((OWNERS, 8, BLOCK), F32),
            vm((OWNERS, CAP, SLOT, HD), BF16), vm((OWNERS, 8, BLOCK), F32),
            vm((CAP, SLOT, OWNERS * 8), F32),
            vm((ROWS * SLOT, rows), F32), vm((ROWS * SLOT, rows), BF16),
            vm((ROWS * SLOT, SUFFIX), F32), vm((ROWS * SLOT, SUFFIX), BF16),
            vm((ROWS * SLOT, HD), F32), vm((ROWS * SLOT, HD), F32), vm((ROWS * SLOT, HD), F32),
            vm((ROWS * SLOT, HD), F32), vm((SUFS, PIECES, HEADS, rows, HD), BF16), vm((rows, WIDTH), F32),
            dma((8,)), dma,
            dma((OWNERS,)), dma((OWNERS,)), dma((OWNERS,)), dma((OWNERS,)),
            dma((OWNERS,)), dma((OWNERS,)), dma((7 * PIECES,)), dma((SUFS, PIECES)),
        ],
        compiler_params=pltpu.CompilerParams(
            collective_id=0, has_side_effects=True, vmem_limit_bytes=58 * 2**20
        ),
    )(
        prompt_of_row, partner, suffix_len,
        queries.reshape(ROWS, STEPS, GROUP, HD).swapaxes(1, 2).reshape(ROWS, SLOT, HD), new_keys.reshape(rows, HD), new_values.reshape(rows, HD),
        suffix_keys, suffix_values,
        prompt_keys.reshape(LENGTH, HD), prompt_values.reshape(LENGTH, HD), out_weight,
    )
    projected = projected.reshape(ROWS, GROUP, STEPS, HD).swapaxes(1, 2)
    return projected.reshape(ROWS, STEPS, WIDTH)


def solution(mesh):
    return jax.shard_map(
        body,
        mesh=mesh,
        in_specs=(
            P("owner", None, "suf"),
            P("owner", None, "suf"),
            P("owner", None, "suf"),
            P("owner", "suf", None, None),
            P("owner", "suf", None, None),
            P("owner", None, "suf"),
            P("owner", None, "suf"),
            P("owner"),
            P("owner"),
            P("owner"),
            P(None, "suf"),
        ),
        out_specs=P("owner", None, "suf"),
        check_vma=False,
    )
```

```python
import jax
import jax.numpy as jnp
from jax import lax
from jax.experimental import pallas as pl
from jax.experimental.pallas import tpu as pltpu
from jax.sharding import PartitionSpec as P

MESH = pl.DeviceIdType.MESH
HD = 128
GROUP = 8
CAP = 8
STEPS = 2
SIDE = 4
OWNERS = 16
SUFS = 8
ROWS = 32
SLOT = STEPS * GROUP
BLOCK = CAP * SLOT
LENGTH = 8192
SUFFIX = 256
WIDTH = GROUP * HD
SPAN = 1024
CHUNK = SIDE * BLOCK
SPANS = LENGTH // SPAN
PIECES = 4
HEADS = GROUP // PIECES
RATE = HD ** (-0.5) * 1.4426950408889634
F32 = jnp.float32
BF16 = jnp.bfloat16


def dot_t(a, b):
    return lax.dot_general(a, b, (((1,), (1,)), ((), ())), preferred_element_type=F32)


STEPS_Y = (0, 0, 1, 3, 2, 2, 1, 3, 2, 2, 1, 3, 0, 0, 1, 3)
STEPS_Z = (0, 2, 1, 3, 1, 3, 3, 1, 0, 2, 2, 2, 1, 3, 0, 0)
OPPOSITE = (0, 1, 3, 2, 5, 4, 7, 6, 8, 9, 11, 10, 13, 12, 15, 14)


def kernel(
    prompt_s, partner_s, length_s,
    q_hbm, nk_hbm, nv_hbm, ks_hbm, vs_hbm, k_hbm, v_hbm, w_hbm,
    out_ref,
    q_v, nk_v, nv_v, ks_v, vs_v, k_v, v_v, vt_v, w_v,
    table_v, table_s, pack_v, rq_v,
    s_v, p_v, top_v, m_v, l_v, acc_v,
    part_v, stat_v, back_v, bstat_v, bstat_t,
    e_v, pe_v, ls_v, lw_v, lo_v, lm_v, lt_v,
    att_v, ag_v, proj_v,
    load_sem, table_sem,
    qsend, qrecv, bsend, brecv, ssend, srecv, gsend, grecv,
):
    me = lax.axis_index("owner")
    mine = lax.axis_index("suf")
    y, z = me // SIDE, me % SIDE
    x, core = mine // 2, mine % 2
    right, left = (x + 1) % SIDE * 2 + core, (x + 3) % SIDE * 2 + core
    across = (x + 2) % SIDE * 2 + core
    sibling = x * 2 + 1 - core

    def owner_at(dy, dz):
        return (y + dy) % SIDE * SIDE + (z + dz) % SIDE

    others = [(i, owner_at(STEPS_Y[i], STEPS_Z[i])) for i in range(1, OWNERS)]

    barrier = pltpu.get_barrier_semaphore()
    for _, t in others:
        pl.semaphore_signal(barrier, inc=1, device_id={"owner": t}, device_id_type=MESH)
    for t in (right, left, sibling):
        pl.semaphore_signal(barrier, inc=1, device_id={"suf": t}, device_id_type=MESH)

    pairs = (
        (q_hbm, q_v), (nk_hbm, nk_v), (nv_hbm, nv_v), (ks_hbm, ks_v), (vs_hbm, vs_v),
        (v_hbm, v_v), (k_hbm, k_v), (w_hbm, w_v),
    )
    loads = [
        pltpu.make_async_copy(src, dst, load_sem.at[i]) for i, (src, dst) in enumerate(pairs)
    ]
    for copy in loads:
        copy.start()
    ld_q, ld_nk, ld_nv, ld_ks, ld_vs, ld_v, ld_k, ld_w = loads

    lane = lax.broadcasted_iota(jnp.int32, (8, 128), 1)
    sub = lax.broadcasted_iota(jnp.int32, (8, 128), 0)
    lane_prompt, lane_place = lane // CAP, lane % CAP
    count = jnp.zeros((8, 128), jnp.int32)
    row_of = jnp.zeros((8, 128), jnp.int32)
    own_prompt = jnp.zeros((8, 128), jnp.int32)
    for r in range(ROWS):
        named = prompt_s[r]
        match = lane_prompt == named
        row_of = jnp.where(match & (count == lane_place), r, row_of)
        count = count + jnp.where(match, 1, 0)
        own_prompt = jnp.where(lane == r, named, own_prompt)
    rank = jnp.zeros((8, 128), jnp.int32)
    for r in range(ROWS):
        rank = rank + jnp.where((own_prompt == prompt_s[r]) & (lane > r), 1, 0)
    table_v[...] = jnp.where(sub == 0, row_of, rank % CAP)
    to_smem = pltpu.make_async_copy(table_v, table_s, table_sem)
    to_smem.start()
    to_smem.wait()
    ld_q.wait()

    def pack(t):
        for u in range(CAP):
            slot = t * CAP + u
            pack_v[pl.ds(pl.multiple_of(slot * SLOT, SLOT), SLOT), :] = q_v[table_s[0, slot]]

    def block_of(i):
        return pl.ds(pl.multiple_of(i * BLOCK, BLOCK), BLOCK)

    pl.semaphore_wait(barrier, OWNERS - 1 + 3)

    def query_copy(t, i, there):
        return pltpu.make_async_remote_copy(
            src_ref=pack_v.at[block_of(t)], dst_ref=rq_v.at[block_of(there)],
            send_sem=qsend.at[i], recv_sem=qrecv.at[there],
            device_id={"owner": t}, device_id_type=MESH,
        )

    for i, t in others:
        pack(t)
        query_copy(t, i, OPPOSITE[i]).start()
    pack(me)
    rq_v[block_of(0), :] = pack_v[block_of(me), :]

    ld_nk.wait()
    ld_nv.wait()
    e_v[...] = dot_t(q_v[...].reshape(ROWS * SLOT, HD), nk_v[...])
    ld_ks.wait()
    ld_vs.wait()
    early = lax.broadcasted_iota(jnp.int32, (SLOT, SUFFIX), 0) % STEPS == 0
    slot_lane = lax.broadcasted_iota(jnp.int32, (SLOT, SUFFIX), 1)
    extra_early = lax.broadcasted_iota(jnp.int32, (SLOT, 2 * ROWS), 0) % STEPS == 0
    extra_lane = lax.broadcasted_iota(jnp.int32, (SLOT, 2 * ROWS), 1)
    part_early = lax.broadcasted_iota(jnp.int32, (SLOT, HD), 0) % STEPS == 0

    def local_scores(r):
        parent = partner_s[r] % ROWS
        rows = pl.ds(pl.multiple_of(r * SLOT, SLOT), SLOT)
        query = q_v[r]
        scores = jnp.where(early, dot_t(query, ks_v[r]), dot_t(query, ks_v[parent]))
        valid = slot_lane < jnp.where(early, length_s[r], length_s[parent])
        ls_v[rows, :] = jnp.where(valid, scores, -1e30)
        one = jnp.where(extra_early, 2 * r, 2 * parent)
        two = jnp.where(extra_early, 2 * r, 2 * r + 1)
        extra_valid = (extra_lane == one) | (extra_lane == two)
        e_v[rows, :] = jnp.where(extra_valid, e_v[rows, :], -1e30)

    def local_weights(i):
        rows = pl.ds(pl.multiple_of(i * BLOCK, BLOCK), BLOCK)
        scores, extra = ls_v[rows, :], e_v[rows, :]
        top = jnp.maximum(
            jnp.max(scores, axis=1, keepdims=True), jnp.max(extra, axis=1, keepdims=True)
        )
        weights = jnp.exp2((scores - top) * RATE)
        extra = jnp.exp2((extra - top) * RATE)
        total = jnp.sum(weights, axis=1, keepdims=True) + jnp.sum(extra, axis=1, keepdims=True)
        lw_v[rows, :] = weights.astype(BF16)
        pe_v[rows, :] = extra.astype(BF16)
        lm_v[rows, :] = jnp.broadcast_to(top, (BLOCK, HD))
        lt_v[rows, :] = jnp.broadcast_to(total, (BLOCK, HD))

    def local_values(r):
        parent = partner_s[r] % ROWS
        rows = pl.ds(pl.multiple_of(r * SLOT, SLOT), SLOT)
        weights = lw_v[rows, :]
        first = jnp.dot(weights, vs_v[r], preferred_element_type=F32)
        second = jnp.dot(weights, vs_v[parent], preferred_element_type=F32)
        lo_v[rows, :] = jnp.where(part_early, first, second)

    def by_eight(step):
        def run(i, carry):
            for u in range(8):
                step(i * 8 + u)
            return carry

        lax.fori_loop(0, ROWS // 8, run, 0)

    by_eight(local_scores)
    for i in range(ROWS * SLOT // BLOCK):
        local_weights(i)
    by_eight(local_values)
    lo_v[...] += jnp.dot(pe_v[...], nv_v[...], preferred_element_type=F32)

    ld_v.wait()

    def turn(i, carry):
        at = pl.ds(pl.multiple_of(i * 512, 512), 512)
        vt_v[:, at] = v_v[at, :].T
        return carry

    lax.fori_loop(0, LENGTH // 512, turn, 0)
    ld_k.wait()
    for i in range(1, 2 * SIDE):
        query_copy(others[0][1], i, i).wait_recv()

    def score(c, j):
        at = pl.ds(pl.multiple_of(c * CHUNK, CHUNK), CHUNK)
        s = dot_t(k_v[j * SPAN:(j + 1) * SPAN, :], rq_v[at, :])
        s_v[j % 2] = s
        top_v[j % 2] = jnp.max(s.reshape(SPAN // 8, 8, CHUNK), axis=0)

    def absorb(j):
        top = jnp.max(top_v[j % 2], axis=0, keepdims=True)
        if j == 0:
            m_new = jnp.broadcast_to(top, (8, CHUNK))
        else:
            m_old = m_v[...]
            m_new = jnp.maximum(m_old, top)
            decay = jnp.exp2((m_old - m_new) * RATE)
        m_v[...] = m_new
        p = jnp.exp2((s_v[j % 2] - m_new[:1]) * RATE)
        total = jnp.sum(p.reshape(SPAN // 8, 8, CHUNK), axis=0)
        p_v[...] = p.astype(BF16)
        term = jnp.dot(
            vt_v[:, j * SPAN:(j + 1) * SPAN], p_v[...], preferred_element_type=F32
        )
        if j == 0:
            l_v[...] = total
            acc_v[...] = term
        else:
            l_v[...] = l_v[...] * decay + total
            acc_v[...] = acc_v[...] * decay[:1] + term

    def part_copy(i, t, source):
        return pltpu.make_async_remote_copy(
            src_ref=part_v.at[i], dst_ref=back_v.at[source],
            send_sem=bsend.at[i], recv_sem=brecv.at[source],
            device_id={"owner": t}, device_id_type=MESH,
        )

    def stat_copy(i, t, source):
        return pltpu.make_async_remote_copy(
            src_ref=stat_v.at[i], dst_ref=bstat_v.at[source],
            send_sem=ssend.at[i], recv_sem=srecv.at[source],
            device_id={"owner": t}, device_id_type=MESH,
        )

    def pick(table, c, k):
        value = table[k]
        for n in range(1, SIDE):
            value = jnp.where(c == n, table[n * SIDE + k], value)
        return value

    score(0, 0)

    def chunk(c, carry):
        @pl.when((c > 0) & (c < SIDE - 1))
        def _():
            for k in range(SIDE):
                query_copy(others[0][1], (c + 1) * SIDE + k, (c + 1) * SIDE + k).wait_recv()

        for j in range(SPANS):
            if j + 1 < SPANS:
                score(c, j + 1)
            else:
                score(jnp.minimum(c + 1, SIDE - 1), 0)
            absorb(j)
        total = jnp.sum(l_v[...], axis=0, keepdims=True)
        top = m_v[:1, :]
        done = acc_v[...] / total
        for k in range(SIDE):
            i = c * SIDE + k
            t = owner_at(pick(STEPS_Y, c, k), pick(STEPS_Z, c, k))
            cols = slice(k * BLOCK, (k + 1) * BLOCK)
            piece = done[:, cols].T.astype(BF16).reshape(CAP, SLOT, HD)
            stats = jnp.concatenate(
                [top[:, cols], total[:, cols], jnp.zeros((6, BLOCK), F32)], axis=0
            )

            @pl.when(i == 0)
            def _():
                back_v[me] = piece
                bstat_v[me] = stats

            @pl.when(i != 0)
            def _():
                part_v[i] = piece
                stat_v[i] = stats
                part_copy(i, t, me).start()
                stat_copy(i, t, me).start()

        return carry

    lax.fori_loop(0, SIDE, chunk, 0)

    for i, t in others:
        part_copy(i, t, t).wait_recv()
        stat_copy(i, t, t).wait_recv()

    bstat_t[...] = bstat_v[...].reshape(OWNERS * 8, BLOCK).T.reshape(CAP, SLOT, OWNERS * 8)
    stat_lane = lax.broadcasted_iota(jnp.int32, (SLOT, OWNERS * 8), 1)

    def merge_row(r):
        named = prompt_s[r]
        rows = pl.ds(pl.multiple_of(r * SLOT, SLOT), SLOT)
        place = table_s[1, r]
        part = back_v[named, place].astype(F32)
        both = bstat_t[place]
        p_max = jnp.sum(jnp.where(stat_lane == named * 8, both, 0.0), axis=1, keepdims=True)
        p_sum = jnp.sum(jnp.where(stat_lane == named * 8 + 1, both, 0.0), axis=1, keepdims=True)
        l_max, l_sum = lm_v[rows, :], lt_v[rows, :]
        top = jnp.maximum(p_max, l_max)
        a = p_sum * jnp.exp2((p_max - top) * RATE)
        b = jnp.exp2((l_max - top) * RATE)
        att_v[rows, :] = (a * part + b * lo_v[rows, :]) / (a + b * l_sum)

    for r in range(ROWS):
        merge_row(r)
    sent = []

    def gather_copy(block, piece, to, i):
        return pltpu.make_async_remote_copy(
            src_ref=ag_v.at[block, piece], dst_ref=ag_v.at[block, piece],
            send_sem=gsend.at[i], recv_sem=grecv.at[block, piece],
            device_id={"suf": to}, device_id_type=MESH,
        )

    def send(block, piece, to):
        copy = gather_copy(block, piece, to, len(sent))
        copy.start()
        sent.append(copy)

    def arrive(block, piece):
        gather_copy(block, piece, sibling, 0).wait_recv()

    def project(block, piece, first=False):
        a = ag_v[block, piece]
        a = jnp.concatenate([a[h] for h in range(HEADS)], axis=1)
        start = block * WIDTH + piece * HEADS * HD
        w = w_v[pl.ds(pl.multiple_of(start, HEADS * HD), HEADS * HD), :]
        term = jnp.dot(a, w, preferred_element_type=F32)
        if first:
            proj_v[...] = term
        else:
            proj_v[...] += term

    def ready(piece):
        for h in range(piece * HEADS, (piece + 1) * HEADS):
            both = [att_v[pl.ds(STEPS * h + s, ROWS, stride=SLOT), :] for s in range(STEPS)]
            ag_v[mine, piece, h % HEADS] = jnp.concatenate(both, axis=0).astype(BF16)

    middle = PIECES // 2
    for p in range(middle):
        ready(p)
        send(mine, p, right)
        ready(middle + p)
        send(mine, middle + p, left)
    for p in range(middle):
        send(mine, middle + p, right)
        send(mine, p, left)
    for p in range(PIECES):
        send(mine, p, sibling)
    ld_w.wait()
    for p in range(PIECES):
        project(mine, p, p == 0)
    for p in range(middle):
        arrive(left, p)
        send(left, p, right)
        send(left, p, sibling)
        arrive(right, middle + p)
        send(right, middle + p, left)
        send(right, middle + p, sibling)
    for p in range(PIECES):
        arrive(sibling, p)
        project(sibling, p)
    for p in range(middle):
        project(left, p)
        project(right, middle + p)
    for p in range(middle):
        arrive(left, middle + p)
        send(left, middle + p, sibling)
        arrive(right, p)
        send(right, p, sibling)
    for p in range(middle):
        project(left, middle + p)
        project(right, p)
    for p in range(middle):
        arrive(across, p)
        send(across, p, sibling)
        arrive(across, middle + p)
        send(across, middle + p, sibling)
    for p in range(PIECES):
        project(across, p)
    turned = 1 - 2 * core
    for p in range(middle):
        for block, piece in ((left, p), (right, middle + p)):
            arrive(block + turned, piece)
            project(block + turned, piece)
    for p in range(middle):
        for block, piece in ((left, middle + p), (right, p)):
            arrive(block + turned, piece)
            project(block + turned, piece)
    for p in range(middle):
        for piece in (p, middle + p):
            arrive(across + turned, piece)
            project(across + turned, piece)

    for j in range(GROUP):
        for s in range(STEPS):
            out_ref[pl.ds(STEPS * j + s, ROWS, stride=SLOT), :] = (
                proj_v[s * ROWS:(s + 1) * ROWS, j * HD:(j + 1) * HD]
            )

    for copy in sent:
        copy.wait_send()
    for i, t in others:
        query_copy(t, i, OPPOSITE[i]).wait_send()
        part_copy(i, t, me).wait_send()
        stat_copy(i, t, me).wait_send()


def body(
    queries, new_keys, new_values, prompt_keys, prompt_values, suffix_keys, suffix_values,
    suffix_len, prompt_of_row, partner, out_weight,
):
    smem = pl.BlockSpec(memory_space=pltpu.SMEM)
    anywhere = pl.BlockSpec(memory_space=pl.ANY)
    vm = pltpu.VMEM
    dma = pltpu.SemaphoreType.DMA
    rows = STEPS * ROWS
    projected = pl.pallas_call(
        kernel,
        out_shape=jax.ShapeDtypeStruct((ROWS * SLOT, HD), F32),
        in_specs=[smem] * 3 + [anywhere] * 8,
        out_specs=pl.BlockSpec(memory_space=pltpu.VMEM),
        scratch_shapes=[
            vm((ROWS, SLOT, HD), BF16), vm((rows, HD), BF16), vm((rows, HD), BF16),
            vm((ROWS, SUFFIX, HD), BF16), vm((ROWS, SUFFIX, HD), BF16),
            vm((LENGTH, HD), BF16), vm((LENGTH, HD), BF16), vm((HD, LENGTH), BF16),
            vm((SUFS * WIDTH, WIDTH), BF16),
            vm((8, 128), jnp.int32), pltpu.SMEM((8, 128), jnp.int32),
            vm((OWNERS * BLOCK, HD), BF16), vm((OWNERS * BLOCK, HD), BF16),
            vm((2, SPAN, CHUNK), F32), vm((SPAN, CHUNK), BF16), vm((2, 8, CHUNK), F32),
            vm((8, CHUNK), F32), vm((8, CHUNK), F32), vm((HD, CHUNK), F32),
            vm((OWNERS, CAP, SLOT, HD), BF16), vm((OWNERS, 8, BLOCK), F32),
            vm((OWNERS, CAP, SLOT, HD), BF16), vm((OWNERS, 8, BLOCK), F32),
            vm((CAP, SLOT, OWNERS * 8), F32),
            vm((ROWS * SLOT, rows), F32), vm((ROWS * SLOT, rows), BF16),
            vm((ROWS * SLOT, SUFFIX), F32), vm((ROWS * SLOT, SUFFIX), BF16),
            vm((ROWS * SLOT, HD), F32), vm((ROWS * SLOT, HD), F32), vm((ROWS * SLOT, HD), F32),
            vm((ROWS * SLOT, HD), F32), vm((SUFS, PIECES, HEADS, rows, HD), BF16), vm((rows, WIDTH), F32),
            dma((8,)), dma,
            dma((OWNERS,)), dma((OWNERS,)), dma((OWNERS,)), dma((OWNERS,)),
            dma((OWNERS,)), dma((OWNERS,)), dma((7 * PIECES,)), dma((SUFS, PIECES)),
        ],
        compiler_params=pltpu.CompilerParams(
            collective_id=0, has_side_effects=True, vmem_limit_bytes=58 * 2**20
        ),
    )(
        prompt_of_row, partner, suffix_len,
        queries.reshape(ROWS, STEPS, GROUP, HD).swapaxes(1, 2).reshape(ROWS, SLOT, HD), new_keys.reshape(rows, HD), new_values.reshape(rows, HD),
        suffix_keys, suffix_values,
        prompt_keys.reshape(LENGTH, HD), prompt_values.reshape(LENGTH, HD), out_weight,
    )
    projected = projected.astype(BF16).reshape(ROWS, GROUP, STEPS, HD).swapaxes(1, 2)
    return projected.reshape(ROWS, STEPS, WIDTH)


def solution(mesh):
    return jax.shard_map(
        body,
        mesh=mesh,
        in_specs=(
            P("owner", None, "suf"),
            P("owner", None, "suf"),
            P("owner", None, "suf"),
            P("owner", "suf", None, None),
            P("owner", "suf", None, None),
            P("owner", None, "suf"),
            P("owner", None, "suf"),
            P("owner"),
            P("owner"),
            P("owner"),
            P(None, "suf"),
        ),
        out_specs=P("owner", None, "suf"),
        check_vma=False,
    )
```
